128 devices in a mesh: island: 8 (over y, z_lo), fsdp: 16 (over z_hi, x, core).
Axes of the slice: x: 4, y: 4, z: 4 (z_hi: 2, z_lo: 2; z = z_hi * 2 + z_lo), core: 2. Of those that a mesh axis runs over, the one named last changes fastest.
Arguments:
- tokens: bfloat16 [98304, 4096], P(('island', 'fsdp')), may hold values from -3 to 3
- key_cotangent: bfloat16 [98304, 1024], P(('island', 'fsdp')), may hold values from -3 to 3
- local_keys: bfloat16 [8, 4, 4096, 1024], P('island', None, 'fsdp'), may hold values from -0.09375 to 0.09375
- pseudo_codes: int32 [8, 4096, 1024], P('island', 'fsdp'), may hold values from -127 to 127
- code_exponents: int32 [8, 4096, 8], P('island', 'fsdp'), may hold values from -15 to -13
- outer_weights: float32 [4096, 1024], P('fsdp'), may hold values from -0.09375 to 0.09375
- outer_momentum: float32 [4096, 1024], P('fsdp'), may hold values from -0.02 to 0.02
- fragment: int32 [8], P('island'), may hold values from 0 to 3
Outputs:
- input_grads: bfloat16 [98304, 4096], P(('island', 'fsdp'))
- weight_grads: bfloat16 [8, 4096, 1024], P('island', 'fsdp')
- new_weights: float32 [4096, 1024], P('fsdp')
- new_momentum: float32 [4096, 1024], P('fsdp')
- synced_keys: bfloat16 [8, 4096, 1024], P('island', 'fsdp')
The draws below stay inside these ranges and needn't reach their ends.
Inputs may be any that keep to these rules, and one draw needn't show every extreme that they name: `fragment`: for each island, an index into the block's layers.
All inputs are finite; a program needn't handle non-finite values.
Results may differ from the reference program's by a relative error of at most 0.019.
Values may be sent and summed in bfloat16 or wider, within the bound.
No kernel may reach another device: no remote copies, remote signals or barrier semaphores. Data moves between devices by JAX's collectives and lax.ppermute only.
A program may use at most 128 MiB of HBM per device.

```python
import jax
import jax.numpy as jnp
from jax import lax

D = 4096
KV = 1024
QB = 128
LAYERS = 4
TOK_DEV = 768
ISLANDS = 8
TOKENS = 98304
N_ISLAND = 8
N_FSDP = 16


def with_ends(values, rng, least, largest):
    place = [jax.random.randint(jax.random.fold_in(rng, axis), (), 0, length) for axis, length in enumerate(values.shape)]
    main_axis = values.shape.index(max(values.shape))
    neighbour = place[:main_axis] + [(place[main_axis] + 1) % values.shape[main_axis]] + place[main_axis + 1:]
    return values.at[tuple(place)].set(least).at[tuple(neighbour)].set(largest)


def with_spikes(drawn, rng, source, target, shards_of, factor):
    def block_of(dim):
        return (jnp.arange(drawn.shape[dim]) // (drawn.shape[dim] // shards_of)).reshape((-1,) + (1,) * (drawn.ndim - 1 - dim))

    near = jax.random.permutation(rng, shards_of)[block_of(target)]
    other_side = (block_of(target) + shards_of // 2) % shards_of
    return jnp.where((block_of(source) == near) | (block_of(source) == other_side), factor * drawn, drawn)


def levels(key, extent, split, smallest, high):
    level = 1.0
    for position, shards_of in split:
        draws = jax.random.uniform(jax.random.fold_in(jax.random.fold_in(key, 6), position), (shards_of,), jnp.float32, smallest / len(split), high / len(split))
        level = level * jnp.repeat(jnp.exp(draws), extent[position] // shards_of).reshape((-1,) + (1,) * (len(extent) - 1 - position))
    return level


def bell_draw(own_key, dims, scale, reach, shards=(), dtype=jnp.bfloat16):
    drawn = jax.random.normal(own_key, dims, jnp.float32) * scale
    if len(shards) > 0:
        drawn = levels(own_key, dims, shards, -0.22, 0.18) * drawn
    return jnp.clip(drawn, min=-reach, max=reach).astype(dtype)


def bell_draw_with(stream_key, shape, width, reach, split, heavy, held_as=jnp.bfloat16):
    result = width * jax.random.normal(stream_key, shape, jnp.float32)
    if split:
        result = result * levels(stream_key, shape, split, -0.22, 0.18)
    return jnp.clip(with_spikes(result, jax.random.fold_in(stream_key, 3), *heavy), -reach, reach).astype(held_as)


def setup_inputs(seed: int = 0) -> dict:
    keys = jax.random.split(jax.random.key(seed), 9)
    tokens = bell_draw_with(keys[0], (TOKENS, D), 0.125, 3.0, ((0, 128),), (0, 1, 128, 5.5))
    key_cotangent = bell_draw(keys[1], (TOKENS, KV), 0.5, 3.0, ((0, 128),))
    local_keys = bell_draw(keys[2], (ISLANDS, LAYERS, D, KV), D ** -0.5, 0.09375, ((0, 8), (2, 16)))
    pseudo_codes = with_ends(jax.random.randint(keys[3], (ISLANDS, D, KV), -127, 128), jax.random.fold_in(keys[3], 1), -127, 127).astype(jnp.int32)
    code_exponents = with_ends(jax.random.randint(keys[4], (ISLANDS, D, KV // QB), -15, -12), jax.random.fold_in(keys[4], 1), -15, (-12) - 1).astype(jnp.int32)
    outer_weights = bell_draw(keys[5], (D, KV), D ** -0.5, 0.09375, ((0, 16),), jnp.float32)
    outer_momentum = bell_draw(keys[6], (D, KV), 0.003, 0.02, ((0, 16),), jnp.float32)
    fragment = with_ends(jax.random.randint(keys[7], (ISLANDS,), 0, LAYERS), jax.random.fold_in(keys[7], 1), 0, LAYERS - 1).astype(jnp.int32)
    return dict(tokens=tokens, key_cotangent=key_cotangent, local_keys=local_keys, pseudo_codes=pseudo_codes, code_exponents=code_exponents, outer_weights=outer_weights, outer_momentum=outer_momentum, fragment=fragment)


momentum_rate = 0.9
outer_rate = 0.7
keep_share = 0.5


def island_pass(operands):
    rows_x, rows_g, key_layer = operands
    flat_g = rows_g.reshape(-1, KV)
    input_part = jnp.dot(flat_g, key_layer.T, preferred_element_type=jnp.float32).astype(jnp.bfloat16)

    def add_group(total, pair):
        group_x, group_g = pair
        partial_term = jnp.dot(group_x.T, group_g, preferred_element_type=jnp.float32).astype(jnp.bfloat16)
        partial_term = lax.optimization_barrier(partial_term)
        return total + partial_term.astype(jnp.float32), None

    total, _ = lax.scan(add_group, jnp.zeros((D, KV), jnp.float32), (rows_x, rows_g))
    return input_part, total.astype(jnp.bfloat16)


def pick_layer(layers, index):
    return lax.dynamic_index_in_dim(layers, index, 0, keepdims=False)


def reference(tokens, key_cotangent, local_keys, pseudo_codes, code_exponents, outer_weights, outer_momentum, fragment):
    split_x = tokens.reshape(N_ISLAND, N_FSDP, TOK_DEV, D)
    split_g = key_cotangent.reshape(N_ISLAND, N_FSDP, TOK_DEV, KV)
    last_layer = local_keys[:, LAYERS - 1]
    input_parts, weight_grads = lax.map(island_pass, (split_x, split_g, last_layer))
    input_grads = input_parts.reshape(TOKENS, D)
    scales = jnp.exp2(code_exponents.astype(jnp.float32))
    scaled_codes = pseudo_codes.reshape(N_ISLAND, D, KV // QB, QB).astype(jnp.float32) * scales[:, :, :, None]
    island_delta = scaled_codes.reshape(N_ISLAND, D, KV)
    mean_delta = jnp.sum(island_delta, axis=0) / N_ISLAND
    new_momentum = momentum_rate * outer_momentum + mean_delta
    new_weights = outer_weights - outer_rate * (mean_delta + momentum_rate * new_momentum)
    chosen = jax.vmap(pick_layer)(local_keys, fragment.astype(jnp.int32))
    synced_keys = (keep_share * chosen.astype(jnp.float32) + (1.0 - keep_share) * new_weights[None]).astype(jnp.bfloat16)
    return input_grads, weight_grads, new_weights, new_momentum, synced_keys
```

```python
import jax
import jax.numpy as jnp
from jax import lax
from jax.experimental import pallas as pl
from jax.experimental.pallas import tpu as pltpu
from jax.sharding import PartitionSpec as P

momentum_rate = 0.9
outer_rate = 0.7
keep_share = 0.5

BLK = 256
PR = 144
QR = BLK - PR
MIB = 1 << 20


def fsdp_perm(move):
    pairs = []
    for h in range(2):
        for x in range(4):
            for c in range(2):
                h2, x2, c2 = move(h, x, c)
                pairs.append((h * 8 + x * 2 + c, (h2 % 2) * 8 + (x2 % 4) * 2 + c2))
    return pairs


def block_at(place, dh, dx):
    return (place ^ (dh << 3)) & 9 | ((((place >> 1) + dx) & 3) << 1)


def to_x(value, step):
    return lax.ppermute(value, "fsdp", fsdp_perm(lambda h, x, c: (h, x + step, c)))


def to_z(value):
    return lax.ppermute(value, "fsdp", fsdp_perm(lambda h, x, c: (h + 1, x, c)))


def to_core(value):
    return lax.ppermute(value, "fsdp", fsdp_perm(lambda h, x, c: (h, x, 1 - c)))


def params(mib):
    return pltpu.CompilerParams(vmem_limit_bytes=mib * MIB)


def term(tok, kc):
    return lax.dot_general(tok, kc, (((0,), (0,)), ((), ())), preferred_element_type=jnp.float32)


def partner_terms(order, tokens, kc):
    rows, width = kc.shape

    def body(order_ref, tok_ref, kc_ref, out_ref):
        out_ref[0] = term(tok_ref[...], kc_ref[...]).astype(jnp.bfloat16)

    return pl.pallas_call(
        body,
        grid_spec=pltpu.PrefetchScalarGridSpec(
            num_scalar_prefetch=1,
            grid=(8,),
            in_specs=[
                pl.BlockSpec((rows, BLK), lambda j, order: (0, block_at(order[0], j >> 2, j & 3))),
                pl.BlockSpec((rows, width), lambda j, order: (0, 0)),
            ],
            out_specs=pl.BlockSpec((1, BLK, width), lambda j, order: (j, 0, 0)),
        ),
        out_shape=jax.ShapeDtypeStruct((8, BLK, width), jnp.bfloat16),
        compiler_params=params(32),
        cost_estimate=pl.CostEstimate(
            flops=2 * 8 * rows * BLK * width, bytes_accessed=9 * MIB, transcendentals=0
        ),
        name="partner_terms",
    )(order, tokens, kc)


def own_terms(order, tokens, kc, received):
    rows, width = kc.shape

    def body(order_ref, tok_ref, kc_ref, got_ref, zp, kp, x1, x2, x3, kq):
        j = pl.program_id(0)
        total = term(tok_ref[...], kc_ref[...]) + got_ref[0].astype(jnp.float32)
        total = total.astype(jnp.bfloat16)
        for k in range(8):
            dh, dx = k // 4, k % 4

            @pl.when(j == k)
            def _():
                (zp if dh else kp)[dx] = total[:PR]
                (kq, x1, x2, x3)[dx][dh] = total[PR:]

    def whole(shape):
        return pl.BlockSpec(shape, lambda j, order: (0,) * len(shape))

    shapes = [(4, PR, width)] * 2 + [(2, QR, width)] * 4
    return pl.pallas_call(
        body,
        grid_spec=pltpu.PrefetchScalarGridSpec(
            num_scalar_prefetch=1,
            grid=(8,),
            in_specs=[
                pl.BlockSpec((rows, BLK), lambda j, order: (0, block_at(order[0], j >> 2, j & 3))),
                whole((rows, width)),
                pl.BlockSpec((1, BLK, width), lambda j, order: (j, 0, 0)),
            ],
            out_specs=[whole(s) for s in shapes],
        ),
        out_shape=[jax.ShapeDtypeStruct(s, jnp.bfloat16) for s in shapes],
        compiler_params=params(40),
        cost_estimate=pl.CostEstimate(
            flops=2 * 8 * rows * BLK * width, bytes_accessed=13 * MIB, transcendentals=0
        ),
        name="own_terms",
    )(order, tokens, kc, received)


def input_part(order, side, kc, blocks, out):
    rows, width = kc.shape
    stacked = len(blocks) == 1

    def body(order_ref, kc_ref, *rest):
        refs, out_ref = rest[: len(blocks)], rest[-1]
        j = pl.program_id(0)

        def product(block):
            out_ref[...] = lax.dot_general(
                kc_ref[...], block, (((1,), (1,)), ((), ())), preferred_element_type=jnp.float32
            ).astype(jnp.bfloat16)

        if stacked:
            product(refs[0][0])
        else:
            for k in range(4):

                @pl.when(j == k)
                def _():
                    product(refs[k][...])

    def whole(shape):
        return pl.BlockSpec(shape, lambda j, order: (0,) * len(shape))

    if stacked:
        block_specs = [pl.BlockSpec((1, BLK, width), lambda j, order: (j, 0, 0))]
    else:
        block_specs = [whole((BLK, width))] * 4
    operands = [order, kc, *blocks]
    in_specs = [whole((rows, width)), *block_specs]
    aliases = {}
    if out is not None:
        aliases = {len(operands): 0}
        operands.append(out)
        in_specs.append(pl.BlockSpec(memory_space=pl.ANY))
    return pl.pallas_call(
        body,
        grid_spec=pltpu.PrefetchScalarGridSpec(
            num_scalar_prefetch=1,
            grid=(4,),
            in_specs=in_specs,
            out_specs=pl.BlockSpec((rows, BLK), lambda j, order: (0, block_at(order[0], side, j))),
        ),
        out_shape=jax.ShapeDtypeStruct((rows, 16 * BLK), jnp.bfloat16),
        input_output_aliases=aliases,
        compiler_params=params(32),
        cost_estimate=pl.CostEstimate(
            flops=2 * 4 * rows * BLK * width, bytes_accessed=5 * MIB, transcendentals=0
        ),
        name="input_part",
    )(*operands)


def stack_rows(groups, width):
    pieces = [(g, start, piece) for g, group in enumerate(groups) for start, piece in group]

    def body(*refs):
        ins, out, sems = refs[: len(pieces)], refs[-2], refs[-1]
        copies = []
        for k, (g, start, piece) in enumerate(pieces):
            copies.append(
                pltpu.make_async_copy(ins[k], out.at[g, pl.ds(start, piece.shape[0])], sems.at[k])
            )
        for copy in copies:
            copy.start()
        for copy in copies:
            copy.wait()

    return pl.pallas_call(
        body,
        in_specs=[pl.BlockSpec(memory_space=pl.ANY)] * len(pieces),
        out_specs=pl.BlockSpec(memory_space=pl.ANY),
        out_shape=jax.ShapeDtypeStruct((len(groups), BLK, width), jnp.bfloat16),
        scratch_shapes=[pltpu.SemaphoreType.DMA((len(pieces),))],
        cost_estimate=pl.CostEstimate(
            flops=0, bytes_accessed=4 * len(groups) * BLK * width, transcendentals=0
        ),
        name="stack_rows",
    )(*[piece for _, _, piece in pieces])


def add_rows(kept, arrived):
    count, rows, width = kept.shape

    def body(a, b, *outs):
        for k in range(count):
            outs[k][...] = (a[k].astype(jnp.float32) + b[k].astype(jnp.float32)).astype(
                jnp.bfloat16
            )

    return pl.pallas_call(
        body,
        out_shape=[jax.ShapeDtypeStruct((rows, width), jnp.bfloat16)] * count,
        compiler_params=params(24),
        cost_estimate=pl.CostEstimate(
            flops=count * rows * width, bytes_accessed=6 * count * rows * width, transcendentals=0
        ),
        name="add_rows",
    )(kept, arrived)


def sum_columns(kept, first, second, third):
    count, rows, width = kept.shape

    def body(a, b, c, d, *outs):
        for k in range(count):
            total = a[k].astype(jnp.float32) + b[k].astype(jnp.float32)
            total = total + c[k].astype(jnp.float32) + d[k].astype(jnp.float32)
            outs[k][...] = total.astype(jnp.bfloat16)

    return pl.pallas_call(
        body,
        out_shape=[jax.ShapeDtypeStruct((rows, width), jnp.bfloat16)] * count,
        compiler_params=params(24),
        cost_estimate=pl.CostEstimate(
            flops=4 * count * rows * width, bytes_accessed=10 * count * rows * width, transcendentals=0
        ),
        name="sum_columns",
    )(kept, first, second, third)


def finish_rows(own, one, two, three, column, arrived):
    width = own.shape[1]

    def body(a, b, c, d, e, f, out):
        total = a[...].astype(jnp.float32) + b[...].astype(jnp.float32)
        total = total + c[...].astype(jnp.float32) + d[...].astype(jnp.float32)
        out[:PR] = total.astype(jnp.bfloat16)
        out[PR:] = (e[...].astype(jnp.float32) + f[...].astype(jnp.float32)).astype(jnp.bfloat16)

    return pl.pallas_call(
        body,
        out_shape=jax.ShapeDtypeStruct((BLK, width), jnp.bfloat16),
        compiler_params=params(24),
        cost_estimate=pl.CostEstimate(
            flops=4 * BLK * width, bytes_accessed=8 * BLK * width, transcendentals=0
        ),
        name="finish_rows",
    )(own, one, two, three, column, arrived)


def local(
    tokens,
    key_cotangent,
    local_keys,
    pseudo_codes,
    code_exponents,
    outer_weights,
    outer_momentum,
    fragment,
):
    place = lax.axis_index("fsdp")
    here = place.astype(jnp.int32).reshape(1)
    there = here ^ 1

    width = key_cotangent.shape[1]

    own = local_keys[0, local_keys.shape[1] - 1]
    left = to_x(own, 1)
    right = to_x(own, -1)
    peer = to_z(own)
    far = to_x(own, 2)

    theirs = partner_terms(there, tokens, key_cotangent)
    theirs = to_core(theirs)
    zp, kp, x1, x2, x3, kq = own_terms(here, tokens, key_cotangent, theirs)

    peer_q = peer[PR:]
    peer_left_q = to_x(peer_q, 1)
    peer_right_q = to_x(peer_q, -1)
    peer_far_q = to_x(peer_q, 2)
    peer_left_p = to_z(left[:PR])
    peer_right_p = to_z(right[:PR])
    peer_far_p = to_z(far[:PR])
    near = [own, right, far, left]
    near_there = to_core(stack_rows([[(0, block)] for block in near], width))
    across = stack_rows(
        [
            [(0, peer)],
            [(0, peer_right_p), (PR, peer_right_q)],
            [(0, peer_far_p), (PR, peer_far_q)],
            [(0, peer_left_p), (PR, peer_left_q)],
        ],
        width,
    )
    across_there = to_core(across)

    grads = input_part(here, 0, key_cotangent, near, None)
    grads = input_part(there, 0, key_cotangent, [near_there], grads)
    grads = input_part(here, 1, key_cotangent, [across], grads)
    input_grads = input_part(there, 1, key_cotangent, [across_there], grads)

    zp = to_z(zp)
    x1 = to_x(x1, 1)
    x3 = to_x(x3, -1)
    x2 = to_x(x2, 2)
    p0, p1, p2, p3 = add_rows(kp, zp)
    p1 = to_x(p1, 1)
    p3 = to_x(p3, -1)
    p2 = to_x(p2, 2)
    q0, q1 = sum_columns(kq, x1, x2, x3)
    q1 = to_z(q1)
    weight_grads = finish_rows(p0, p1, p2, p3, q0, q1)[None]

    row_count = own.shape[0]
    islands = lax.axis_size("island")
    scales = jnp.exp2(code_exponents[0].astype(jnp.float32))
    scaled_codes = (
        pseudo_codes[0].reshape(row_count, scales.shape[1], -1).astype(jnp.float32)
        * scales[:, :, None]
    )
    island_delta = scaled_codes.reshape(islands, row_count // islands, -1).astype(jnp.bfloat16)
    spread = lax.all_to_all(island_delta, "island", 0, 0, tiled=True)
    part = jnp.sum(spread.astype(jnp.float32), axis=0).astype(jnp.bfloat16)
    part = jnp.broadcast_to(part[None], island_delta.shape)
    total = lax.all_to_all(part, "island", 0, 0, tiled=True).reshape(row_count, -1)
    mean_delta = total.astype(jnp.float32) / islands
    new_momentum = momentum_rate * outer_momentum + mean_delta
    new_weights = outer_weights - outer_rate * (mean_delta + momentum_rate * new_momentum)
    chosen = lax.dynamic_index_in_dim(local_keys[0], fragment[0], 0, keepdims=False)
    synced_keys = (
        keep_share * chosen.astype(jnp.float32) + (1.0 - keep_share) * new_weights
    ).astype(jnp.bfloat16)[None]
    return (input_grads, weight_grads, new_weights, new_momentum, synced_keys)


def solution(mesh):
    placed = (
        P(("island", "fsdp"), None),
        P(("island", "fsdp"), None),
        P("island", None, "fsdp", None),
        P("island", "fsdp", None),
        P("island", "fsdp", None),
        P("fsdp", None),
        P("fsdp", None),
        P("island"),
    )
    return jax.shard_map(
        local,
        mesh=mesh,
        in_specs=placed,
        out_specs=(
            P(("island", "fsdp"), None),
            P("island", "fsdp", None),
            P("fsdp", None),
            P("fsdp", None),
            P("island", "fsdp", None),
        ),
        check_vma=False,
    )
```

```python
import jax
import jax.numpy as jnp
from jax import lax
from jax.experimental import pallas as pl
from jax.experimental.pallas import tpu as pltpu
from jax.sharding import PartitionSpec as P

momentum_rate = 0.9
outer_rate = 0.7
keep_share = 0.5

ISLANDS = 8
BLK = 256
MIB = 1 << 20
TERM_MIB = 58
INPUT_MIB = 24
COST = 0.3


def fsdp_perm(move):
    pairs = []
    for h in range(2):
        for x in range(4):
            for c in range(2):
                h2, x2, c2 = move(h, x, c)
                pairs.append((h * 8 + x * 2 + c, (h2 % 2) * 8 + (x2 % 4) * 2 + c2))
    return pairs


def block_at(place, dh, dx):
    return (place ^ (dh << 3)) & 9 | ((((place >> 1) + dx) & 3) << 1)


def to_x(value, step):
    return lax.ppermute(value, "fsdp", fsdp_perm(lambda h, x, c: (h, x + step, c)))


def to_z(value):
    return lax.ppermute(value, "fsdp", fsdp_perm(lambda h, x, c: (h + 1, x, c)))


def to_island(value, move):
    pairs = []
    for y in range(4):
        for side in range(2):
            y2, side2 = move(y, side)
            pairs.append((y * 2 + side, (y2 % 4) * 2 + side2))
    return lax.ppermute(value, "island", pairs)


def to_y(value, step):
    return to_island(value, lambda y, side: (y + step, side))


def to_side(value):
    return to_island(value, lambda y, side: (y, 1 - side))


def to_core(value):
    return lax.ppermute(value, "fsdp", fsdp_perm(lambda h, x, c: (h, x, 1 - c)))


def after(value, earlier):
    return lax.optimization_barrier((value, earlier))[0]


def phase(*values):
    return lax.optimization_barrier(values)


def cost(flops, size):
    return pl.CostEstimate(
        flops=int(flops * COST), bytes_accessed=int(size * COST), transcendentals=0
    )


def params(mib):
    return pltpu.CompilerParams(vmem_limit_bytes=mib * MIB)


def term(tok, kc):
    return lax.dot_general(tok, kc, (((0,), (0,)), ((), ())), preferred_element_type=jnp.float32)


def chip_terms(order, side, tokens, kc, their_tokens, their_kc):
    rows, width = kc.shape

    def body(order_ref, tok_ref, kc_ref, their_tok_ref, their_kc_ref, *rest):
        outs, held, sems = rest[:4], rest[4], rest[5]
        j = pl.program_id(0)
        total = term(tok_ref[...], kc_ref[...])
        total += term(their_tok_ref[...], their_kc_ref[...])
        total = total.astype(jnp.bfloat16)
        for k in range(4):

            @pl.when(j == k)
            def _():
                held[k] = total
                pltpu.make_async_copy(held.at[k], outs[k], sems.at[k]).start()

        @pl.when(j == 3)
        def _():
            for k in range(4):
                pltpu.make_async_copy(held.at[k], outs[k], sems.at[k]).wait()

    whole = pl.BlockSpec((rows, width), lambda j, order: (0, 0))
    columns = pl.BlockSpec((rows, BLK), lambda j, order: (0, block_at(order[0], side, j)))
    return pl.pallas_call(
        body,
        grid_spec=pltpu.PrefetchScalarGridSpec(
            num_scalar_prefetch=1,
            grid=(4,),
            in_specs=[columns, whole, columns, whole],
            out_specs=[pl.BlockSpec(memory_space=pl.ANY)] * 4,
            scratch_shapes=[
                pltpu.VMEM((4, BLK, width), jnp.bfloat16),
                pltpu.SemaphoreType.DMA((4,)),
            ],
        ),
        out_shape=[jax.ShapeDtypeStruct((BLK, width), jnp.bfloat16)] * 4,
        compiler_params=params(TERM_MIB),
        cost_estimate=cost(2 * 8 * rows * BLK * width, 12 * MIB),
        name="chip_terms",
    )(order, tokens, kc, their_tokens, their_kc)


def walk(j):
    return j ^ (j >> 1)


def side_products(order, side, first, kc, their_kc, blocks, grads):
    rows, width = kc.shape
    count = len(blocks)

    def body(order_ref, kc_ref, their_kc_ref, *rest):
        out_ref, theirs_ref = rest[-2:]
        j = pl.program_id(0)
        for k in range(count):

            @pl.when(j == k)
            def _():
                block = rest[k][...]
                for kc_rows, ref in ((kc_ref, out_ref), (their_kc_ref, theirs_ref.at[0])):
                    ref[...] = lax.dot_general(
                        kc_rows[...],
                        block,
                        (((1,), (1,)), ((), ())),
                        preferred_element_type=jnp.float32,
                    ).astype(jnp.bfloat16)

    def whole(shape):
        return pl.BlockSpec(shape, lambda j, order: (0,) * len(shape))

    operands = [order, kc, their_kc, *blocks]
    in_specs = [whole((rows, width))] * 2 + [whole((BLK, width))] * count
    aliases = {}
    if grads is not None:
        aliases = {len(operands): 0}
        operands.append(grads)
        in_specs.append(pl.BlockSpec(memory_space=pl.ANY))
    return pl.pallas_call(
        body,
        grid_spec=pltpu.PrefetchScalarGridSpec(
            num_scalar_prefetch=1,
            grid=(count,),
            in_specs=in_specs,
            out_specs=[
                pl.BlockSpec(
                    (rows, BLK), lambda j, order: (0, block_at(order[0], side, walk(first + j)))
                ),
                pl.BlockSpec((1, rows, BLK), lambda j, order: (j, 0, 0)),
            ],
        ),
        out_shape=[
            jax.ShapeDtypeStruct((rows, 16 * BLK), jnp.bfloat16),
            jax.ShapeDtypeStruct((count, rows, BLK), jnp.bfloat16),
        ],
        input_output_aliases=aliases,
        compiler_params=params(INPUT_MIB),
        cost_estimate=cost(4 * count * rows * BLK * width, 2 * count * MIB),
        name="side_products",
    )(*operands)


def put_blocks(order, grads, *arrived):
    counts = [part.shape[0] for part in arrived]
    pieces = [(group, k) for group, count in enumerate(counts) for k in range(count)]

    def body(order_ref, *rest):
        out_ref, sems = rest[-2:]
        copies = []
        for n, (group, k) in enumerate(pieces):
            place = block_at(order_ref[0] ^ 1, n // 4, walk(n % 4))
            copies.append(
                pltpu.make_async_copy(
                    rest[group].at[k],
                    out_ref.at[:, pl.ds(pl.multiple_of(place * BLK, BLK), BLK)],
                    sems.at[n],
                )
            )
        for copy in copies:
            copy.start()
        for copy in copies:
            copy.wait()

    return pl.pallas_call(
        body,
        grid_spec=pltpu.PrefetchScalarGridSpec(
            num_scalar_prefetch=1,
            grid=(1,),
            in_specs=[
                *[pl.BlockSpec(part.shape, lambda j, order: (0, 0, 0)) for part in arrived],
                pl.BlockSpec(memory_space=pl.ANY),
            ],
            out_specs=pl.BlockSpec(memory_space=pl.ANY),
            scratch_shapes=[pltpu.SemaphoreType.DMA((len(pieces),))],
        ),
        out_shape=jax.ShapeDtypeStruct(grads.shape, jnp.bfloat16),
        input_output_aliases={1 + len(arrived): 0},
        compiler_params=params(INPUT_MIB),
        cost_estimate=cost(0, 6 * MIB),
        name="put_blocks",
    )(order, *arrived, grads)


def dequantize(codes, exponents):
    rows, blocks = exponents.shape
    size = codes.shape[1] // blocks

    def body(codes_ref, exponents_ref, out_ref):
        scales = jnp.exp2(exponents_ref[...].astype(jnp.float32))
        for k in range(blocks):
            part = codes_ref[:, k * size : (k + 1) * size].astype(jnp.float32)
            out_ref[:, k * size : (k + 1) * size] = (part * scales[:, k : k + 1]).astype(
                jnp.bfloat16
            )

    return pl.pallas_call(
        body,
        out_shape=jax.ShapeDtypeStruct(codes.shape, jnp.bfloat16),
        compiler_params=params(INPUT_MIB),
        cost_estimate=cost(2 * rows * codes.shape[1], 2 * MIB),
        name="dequantize",
    )(codes, exponents)


def add_blocks(*blocks):
    rows, width = blocks[0].shape
    step = rows // 2

    def body(*refs):
        total = refs[0][...].astype(jnp.float32)
        for ref in refs[1:-1]:
            total = total + ref[...].astype(jnp.float32)
        refs[-1][...] = total.astype(jnp.bfloat16)

    spec = pl.BlockSpec((step, width), lambda j: (j, 0))
    return pl.pallas_call(
        body,
        grid=(2,),
        in_specs=[spec] * len(blocks),
        out_specs=spec,
        out_shape=jax.ShapeDtypeStruct((rows, width), jnp.bfloat16),
        compiler_params=params(INPUT_MIB),
        cost_estimate=cost(len(blocks) * rows * width, 2 * (len(blocks) + 1) * rows * width),
        name="add_blocks",
    )(*blocks)


def local(
    tokens,
    key_cotangent,
    local_keys,
    pseudo_codes,
    code_exponents,
    outer_weights,
    outer_momentum,
    fragment,
):
    place = lax.axis_index("fsdp")
    here = place.astype(jnp.int32).reshape(1)

    own = local_keys[0, local_keys.shape[1] - 1]
    their_kc = to_core(key_cotangent)
    their_tokens = to_core(tokens)
    left = to_x(own, 1)
    right = to_x(own, -1)
    peer = to_z(own)
    delta = dequantize(pseudo_codes[0], after(code_exponents[0], own))
    far = to_x(after(own, (delta, their_kc)), 2)
    other_delta = to_side(delta)

    away = chip_terms(here, 1, tokens, key_cotangent, their_tokens, after(their_kc, delta))
    left, right, peer, delta = after((left, right, peer, delta), away[0])

    away_one = to_x(away[1], 1)
    away_three = to_x(away[3], -1)
    peer_left = to_z(left)
    home = chip_terms(here, 0, tokens, key_cotangent, their_tokens, after(their_kc, (peer, right)))
    pair = add_blocks(after(delta, home[0]), other_delta)
    away, away_one, away_three, peer_left, pair, home, far, own, right = phase(
        away, away_one, away_three, peer_left, pair, home, far, own, right
    )

    away_two = to_x(away[2], 2)
    peer_right = to_z(right)
    pair_next = to_y(pair, 1)
    pair_last = to_y(pair, -1)
    near = [own, right, left, far]
    grads, near_theirs = side_products(here, 0, 0, key_cotangent, their_kc, near, None)
    away, away_two, peer_right, pair, pair_next, pair_last, grads, near_theirs, home, far = phase(
        away, away_two, peer_right, pair, pair_next, pair_last, grads, near_theirs, home, far
    )

    home_one = to_x(home[1], 1)
    home_three = to_x(home[3], -1)
    peer_far = to_z(far)
    near_there = to_core(near_theirs)
    pair_far = to_y(pair, 2)
    away_sum = add_blocks(away[0], away_one, away_two, away_three)
    across = after([peer, peer_right, peer_left], away_sum)
    grads, across_theirs = side_products(here, 1, 0, key_cotangent, their_kc, across, grads)
    home_one, home_three, peer_far, near_there, pair_far, away_sum, grads, across_theirs, home = phase(
        home_one, home_three, peer_far, near_there, pair_far, away_sum, grads, across_theirs, home
    )

    home_two = to_x(home[2], 2)
    crossed = to_z(away_sum)
    across_there = to_core(across_theirs)
    grads, last_theirs = side_products(here, 1, 3, key_cotangent, their_kc, [peer_far], grads)
    last_there = to_core(last_theirs)
    pairs = (after(pair, grads), pair_next, pair_last, pair_far)
    mean_delta = sum(part.astype(jnp.float32) for part in pairs) / ISLANDS
    new_momentum = momentum_rate * outer_momentum + mean_delta
    new_weights = outer_weights - outer_rate * (mean_delta + momentum_rate * new_momentum)
    chosen = lax.dynamic_index_in_dim(local_keys[0], fragment[0], 0, keepdims=False)
    synced_keys = (
        keep_share * chosen.astype(jnp.float32) + (1.0 - keep_share) * new_weights
    ).astype(jnp.bfloat16)[None]
    input_grads = put_blocks(
        here, after(grads, synced_keys), near_there, across_there, last_there
    )
    home_kept = after(home[0], (input_grads, synced_keys))
    weight_grads = add_blocks(home_kept, home_one, home_two, home_three, crossed)[None]
    return (input_grads, weight_grads, new_weights, new_momentum, synced_keys)


def solution(mesh):
    placed = (
        P(("island", "fsdp"), None),
        P(("island", "fsdp"), None),
        P("island", None, "fsdp", None),
        P("island", "fsdp", None),
        P("island", "fsdp", None),
        P("fsdp", None),
        P("fsdp", None),
        P("island"),
    )
    return jax.shard_map(
        local,
        mesh=mesh,
        in_specs=placed,
        out_specs=(
            P(("island", "fsdp"), None),
            P("island", "fsdp", None),
            P("fsdp", None),
            P("fsdp", None),
            P("island", "fsdp", None),
        ),
        check_vma=False,
    )
```

```python
import jax
import jax.numpy as jnp
from jax import lax
from jax.experimental import pallas as pl
from jax.experimental.pallas import tpu as pltpu
from jax.sharding import PartitionSpec as P

momentum_rate = 0.9
outer_rate = 0.7
keep_share = 0.5

ISLANDS = 8
BLK = 256
HALF = BLK // 2
MIB = 1 << 20
TERM_MIB = 58
INPUT_MIB = 24
COST = 0.3


def fsdp_perm(move):
    pairs = []
    for h in range(2):
        for x in range(4):
            for c in range(2):
                h2, x2, c2 = move(h, x, c)
                pairs.append((h * 8 + x * 2 + c, (h2 % 2) * 8 + (x2 % 4) * 2 + c2))
    return pairs


def block_at(place, dh, dx):
    return (place ^ (dh << 3)) & 9 | ((((place >> 1) + dx) & 3) << 1)


def to_x(value, step):
    return lax.ppermute(value, "fsdp", fsdp_perm(lambda h, x, c: (h, x + step, c)))


def to_z(value):
    return lax.ppermute(value, "fsdp", fsdp_perm(lambda h, x, c: (h + 1, x, c)))


def to_island(value, move):
    pairs = []
    for y in range(4):
        for side in range(2):
            y2, side2 = move(y, side)
            pairs.append((y * 2 + side, (y2 % 4) * 2 + side2))
    return lax.ppermute(value, "island", pairs)


def over_y(copies):
    groups = [[y * 2 + side for y in range(4)] for side in range(2)]
    return lax.all_to_all(copies, "island", 0, 0, axis_index_groups=groups, tiled=True)


def to_side(value):
    return to_island(value, lambda y, side: (y, 1 - side))


def to_core(value):
    return lax.ppermute(value, "fsdp", fsdp_perm(lambda h, x, c: (h, x, 1 - c)))


def after(value, earlier):
    return lax.optimization_barrier((value, earlier))[0]


def phase(*values):
    return lax.optimization_barrier(values)


def cost(flops, size):
    return pl.CostEstimate(
        flops=int(flops * COST), bytes_accessed=int(size * COST), transcendentals=0
    )


def params(mib):
    return pltpu.CompilerParams(vmem_limit_bytes=mib * MIB)


def term(tok, kc):
    return lax.dot_general(tok, kc, (((0,), (0,)), ((), ())), preferred_element_type=jnp.float32)


def chip_terms(order, side, tokens, kc, their_tokens, their_kc):
    rows, width = kc.shape
    pieces = [(0, 0, BLK), (1, 0, BLK), (2, 0, HALF), (2, HALF, HALF), (3, 0, BLK)]
    count = len(pieces)

    def body(order_ref, tok_ref, kc_ref, their_tok_ref, their_kc_ref, *rest):
        outs, held, sems = rest[:count], rest[count], rest[count + 1]

        def copies(block):
            return [
                pltpu.make_async_copy(held.at[k, pl.ds(start, size)], outs[n], sems.at[n])
                for n, (k, start, size) in enumerate(pieces)
                if block is None or k == block
            ]

        j = pl.program_id(0)
        total = term(tok_ref[...], kc_ref[...])
        total += term(their_tok_ref[...], their_kc_ref[...])
        total = total.astype(jnp.bfloat16)
        for k in range(4):

            @pl.when(j == k)
            def _():
                held[k] = total
                for copy in copies(k):
                    copy.start()

        @pl.when(j == 3)
        def _():
            for copy in copies(None):
                copy.wait()

    whole = pl.BlockSpec((rows, width), lambda j, order: (0, 0))
    columns = pl.BlockSpec((rows, BLK), lambda j, order: (0, block_at(order[0], side, j)))
    return pl.pallas_call(
        body,
        grid_spec=pltpu.PrefetchScalarGridSpec(
            num_scalar_prefetch=1,
            grid=(4,),
            in_specs=[columns, whole, columns, whole],
            out_specs=[pl.BlockSpec(memory_space=pl.ANY)] * count,
            scratch_shapes=[
                pltpu.VMEM((4, BLK, width), jnp.bfloat16),
                pltpu.SemaphoreType.DMA((count,)),
            ],
        ),
        out_shape=[jax.ShapeDtypeStruct((size, width), jnp.bfloat16) for _, _, size in pieces],
        compiler_params=params(TERM_MIB),
        cost_estimate=cost(2 * 8 * rows * BLK * width, 12 * MIB),
        name="chip_terms",
    )(order, tokens, kc, their_tokens, their_kc)


def walk(j):
    return j ^ (j >> 1)


def side_products(order, side, first, kc, their_kc, blocks, grads):
    rows, width = kc.shape
    count = len(blocks)

    def body(order_ref, kc_ref, their_kc_ref, *rest):
        out_ref, theirs_ref = rest[-2:]
        j = pl.program_id(0)
        for k in range(count):

            @pl.when(j == k)
            def _():
                block = rest[k][...]
                for kc_rows, ref in ((kc_ref, out_ref), (their_kc_ref, theirs_ref.at[0])):
                    ref[...] = lax.dot_general(
                        kc_rows[...],
                        block,
                        (((1,), (1,)), ((), ())),
                        preferred_element_type=jnp.float32,
                    ).astype(jnp.bfloat16)

    def whole(shape):
        return pl.BlockSpec(shape, lambda j, order: (0,) * len(shape))

    operands = [order, kc, their_kc, *blocks]
    in_specs = [whole((rows, width))] * 2 + [whole((BLK, width))] * count
    aliases = {}
    if grads is not None:
        aliases = {len(operands): 0}
        operands.append(grads)
        in_specs.append(pl.BlockSpec(memory_space=pl.ANY))
    return pl.pallas_call(
        body,
        grid_spec=pltpu.PrefetchScalarGridSpec(
            num_scalar_prefetch=1,
            grid=(count,),
            in_specs=in_specs,
            out_specs=[
                pl.BlockSpec(
                    (rows, BLK), lambda j, order: (0, block_at(order[0], side, walk(first + j)))
                ),
                pl.BlockSpec((1, rows, BLK), lambda j, order: (j, 0, 0)),
            ],
        ),
        out_shape=[
            jax.ShapeDtypeStruct((rows, 16 * BLK), jnp.bfloat16),
            jax.ShapeDtypeStruct((count, rows, BLK), jnp.bfloat16),
        ],
        input_output_aliases=aliases,
        compiler_params=params(INPUT_MIB),
        cost_estimate=cost(4 * count * rows * BLK * width, 2 * count * MIB),
        name="side_products",
    )(*operands)


def put_blocks(order, grads, *arrived):
    counts = [part.shape[0] for part in arrived]
    pieces = [(group, k) for group, count in enumerate(counts) for k in range(count)]

    def body(order_ref, *rest):
        out_ref, sems = rest[-2:]
        copies = []
        for n, (group, k) in enumerate(pieces):
            place = block_at(order_ref[0] ^ 1, n // 4, walk(n % 4))
            copies.append(
                pltpu.make_async_copy(
                    rest[group].at[k],
                    out_ref.at[:, pl.ds(pl.multiple_of(place * BLK, BLK), BLK)],
                    sems.at[n],
                )
            )
        for copy in copies:
            copy.start()
        for copy in copies:
            copy.wait()

    return pl.pallas_call(
        body,
        grid_spec=pltpu.PrefetchScalarGridSpec(
            num_scalar_prefetch=1,
            grid=(1,),
            in_specs=[
                *[pl.BlockSpec(part.shape, lambda j, order: (0, 0, 0)) for part in arrived],
                pl.BlockSpec(memory_space=pl.ANY),
            ],
            out_specs=pl.BlockSpec(memory_space=pl.ANY),
            scratch_shapes=[pltpu.SemaphoreType.DMA((len(pieces),))],
        ),
        out_shape=jax.ShapeDtypeStruct(grads.shape, jnp.bfloat16),
        input_output_aliases={1 + len(arrived): 0},
        compiler_params=params(INPUT_MIB),
        cost_estimate=cost(0, 6 * MIB),
        name="put_blocks",
    )(order, *arrived, grads)


def dequantize(codes, exponents):
    rows, blocks = exponents.shape
    size = codes.shape[1] // blocks

    def body(codes_ref, exponents_ref, out_ref):
        scales = jnp.exp2(exponents_ref[...].astype(jnp.float32))
        for k in range(blocks):
            part = codes_ref[:, k * size : (k + 1) * size].astype(jnp.float32)
            out_ref[:, k * size : (k + 1) * size] = (part * scales[:, k : k + 1]).astype(
                jnp.bfloat16
            )

    return pl.pallas_call(
        body,
        out_shape=jax.ShapeDtypeStruct(codes.shape, jnp.bfloat16),
        compiler_params=params(INPUT_MIB),
        cost_estimate=cost(2 * rows * codes.shape[1], 2 * MIB),
        name="dequantize",
    )(codes, exponents)


def add_blocks(*blocks):
    rows, width = blocks[0].shape
    step = rows // 2

    def body(*refs):
        total = refs[0][...].astype(jnp.float32)
        for ref in refs[1:-1]:
            total = total + ref[...].astype(jnp.float32)
        refs[-1][...] = total.astype(jnp.bfloat16)

    spec = pl.BlockSpec((step, width), lambda j: (j, 0))
    return pl.pallas_call(
        body,
        grid=(2,),
        in_specs=[spec] * len(blocks),
        out_specs=spec,
        out_shape=jax.ShapeDtypeStruct((rows, width), jnp.bfloat16),
        compiler_params=params(INPUT_MIB),
        cost_estimate=cost(len(blocks) * rows * width, 2 * (len(blocks) + 1) * rows * width),
        name="add_blocks",
    )(*blocks)


def plain_kernel(body, shapes, name, *operands):
    return pl.pallas_call(
        body,
        out_shape=[jax.ShapeDtypeStruct(shape, jnp.bfloat16) for shape in shapes],
        compiler_params=params(INPUT_MIB),
        cost_estimate=cost(0, 6 * MIB),
        name=name,
    )(*operands)


def rounded_sum(*parts):
    total = parts[0].astype(jnp.float32)
    for part in parts[1:]:
        total = total + part.astype(jnp.float32)
    return total.astype(jnp.bfloat16)


def pair_copies(own, other):
    rows, width = own.shape

    def body(own_ref, other_ref, out_ref):
        total = rounded_sum(own_ref[...], other_ref[...])
        for k in range(4):
            out_ref[k] = total

    return plain_kernel(body, [(4, rows, width)], "pair_copies", own, other)[0]


def relay_away(one, three, from_left, from_right, low, high):
    width = one.shape[1]

    def body(one_ref, three_ref, left_ref, right_ref, low_ref, high_ref, plus_ref, minus_ref):
        plus_ref[:HALF] = rounded_sum(one_ref[:HALF], left_ref[...])
        plus_ref[HALF:BLK] = one_ref[HALF:]
        plus_ref[BLK:] = low_ref[...]
        minus_ref[:HALF] = three_ref[:HALF]
        minus_ref[HALF:BLK] = rounded_sum(three_ref[HALF:], right_ref[...])
        minus_ref[BLK:] = high_ref[...]

    shapes = [(BLK + HALF, width)] * 2
    return plain_kernel(
        body, shapes, "relay_away", one, three, from_left, from_right, low, high
    )


def relay_home(kept, from_left, from_right, one, three):
    width = kept.shape[1]

    def body(kept_ref, left_ref, right_ref, one_ref, three_ref, sum_ref, plus_ref, minus_ref):
        sum_ref[...] = rounded_sum(kept_ref[...], left_ref[:BLK], right_ref[:BLK])
        plus_ref[:HALF] = rounded_sum(one_ref[:HALF], left_ref[BLK:])
        plus_ref[HALF:] = one_ref[HALF:]
        minus_ref[:HALF] = three_ref[:HALF]
        minus_ref[HALF:] = rounded_sum(three_ref[HALF:], right_ref[BLK:])

    return plain_kernel(
        body, [(BLK, width)] * 3, "relay_home", kept, from_left, from_right, one, three
    )


def local(
    tokens,
    key_cotangent,
    local_keys,
    pseudo_codes,
    code_exponents,
    outer_weights,
    outer_momentum,
    fragment,
):
    place = lax.axis_index("fsdp")
    here = place.astype(jnp.int32).reshape(1)

    own = local_keys[0, local_keys.shape[1] - 1]
    their_kc = to_core(key_cotangent)
    their_tokens = to_core(tokens)
    left = to_x(own, 1)
    right = to_x(own, -1)
    peer = to_z(own)
    delta = dequantize(pseudo_codes[0], after(code_exponents[0], own))
    far = to_x(after(own, (delta, their_kc)), 2)
    other_delta = to_side(delta)

    away = chip_terms(here, 1, tokens, key_cotangent, their_tokens, after(their_kc, delta))
    left, right, peer, delta = after((left, right, peer, delta), away[0])

    low, high = after((away[2], away[3]), (left, right, peer))
    from_left = to_x(low, 1)
    from_right = to_x(high, -1)
    peer_left = to_z(left)
    home = chip_terms(here, 0, tokens, key_cotangent, their_tokens, after(their_kc, (peer, right)))
    peer_right = to_z(after(right, (home[0], peer_left)))
    from_left, from_right, away, home, far, own, other_delta = phase(
        from_left, from_right, away, home, far, own, other_delta
    )
    plus, minus = relay_away(away[1], away[4], from_left, from_right, home[2], home[3])

    away_left = to_x(plus, 1)
    away_right = to_x(minus, -1)
    peer_far = to_z(after(far, peer_left))
    pairs = over_y(pair_copies(after(delta, plus), other_delta))
    near = [own, right, left, far]
    grads, near_theirs = side_products(
        here, 0, 0, key_cotangent, after(their_kc, plus), near, None
    )
    away_left, away_right, peer_right, grads, near_theirs = phase(
        away_left, away_right, peer_right, grads, near_theirs
    )

    away_sum, plus, minus = relay_home(away[0], away_left, away_right, home[1], home[4])
    home_left = to_x(plus, 1)
    home_right = to_x(minus, -1)
    crossed = to_z(away_sum)
    near_there = to_core(after(near_theirs, peer_far))
    across = after([peer, peer_right, peer_left, peer_far], away_sum)
    grads, across_theirs = side_products(here, 1, 0, key_cotangent, their_kc, across, grads)
    across_there = to_core(after(across_theirs, (home_left, home_right, crossed)))
    pairs = after(pairs, grads)
    mean_delta = jnp.sum(pairs.astype(jnp.float32), axis=0) / ISLANDS
    new_momentum = momentum_rate * outer_momentum + mean_delta
    new_weights = outer_weights - outer_rate * (mean_delta + momentum_rate * new_momentum)
    chosen = lax.dynamic_index_in_dim(local_keys[0], fragment[0], 0, keepdims=False)
    synced_keys = (
        keep_share * chosen.astype(jnp.float32) + (1.0 - keep_share) * new_weights
    ).astype(jnp.bfloat16)[None]
    input_grads = put_blocks(here, after(grads, synced_keys), near_there, across_there)
    home_kept = after(home[0], input_grads)
    weight_grads = add_blocks(home_kept, home_left, home_right, crossed)[None]
    return (input_grads, weight_grads, new_weights, new_momentum, synced_keys)


def solution(mesh):
    placed = (
        P(("island", "fsdp"), None),
        P(("island", "fsdp"), None),
        P("island", None, "fsdp", None),
        P("island", "fsdp", None),
        P("island", "fsdp", None),
        P("fsdp", None),
        P("fsdp", None),
        P("island"),
    )
    return jax.shard_map(
        local,
        mesh=mesh,
        in_specs=placed,
        out_specs=(
            P(("island", "fsdp"), None),
            P("island", "fsdp", None),
            P("fsdp", None),
            P("fsdp", None),
            P("island", "fsdp", None),
        ),
        check_vma=False,
    )
```

```python
import jax
import jax.numpy as jnp
from jax import lax
from jax.experimental import pallas as pl
from jax.experimental.pallas import tpu as pltpu
from jax.sharding import PartitionSpec as P

momentum_rate = 0.9
outer_rate = 0.7
keep_share = 0.5

ISLANDS = 8
BLK = 256
HALF = BLK // 2
MIB = 1 << 20
TERM_MIB = 24
INPUT_MIB = 24
COST = 0.3


def fsdp_perm(move):
    pairs = []
    for h in range(2):
        for x in range(4):
            for c in range(2):
                h2, x2, c2 = move(h, x, c)
                pairs.append((h * 8 + x * 2 + c, (h2 % 2) * 8 + (x2 % 4) * 2 + c2))
    return pairs


def block_at(place, dh, dx):
    return (place ^ (dh << 3)) & 9 | ((((place >> 1) + dx) & 3) << 1)


def to_x(value, step):
    return lax.ppermute(value, "fsdp", fsdp_perm(lambda h, x, c: (h, x + step, c)))


def to_z(value):
    return lax.ppermute(value, "fsdp", fsdp_perm(lambda h, x, c: (h + 1, x, c)))


def to_island(value, move):
    pairs = []
    for y in range(4):
        for side in range(2):
            y2, side2 = move(y, side)
            pairs.append((y * 2 + side, (y2 % 4) * 2 + side2))
    return lax.ppermute(value, "island", pairs)


def over_y(copies):
    groups = [[y * 2 + side for y in range(4)] for side in range(2)]
    return lax.all_to_all(copies, "island", 0, 0, axis_index_groups=groups, tiled=True)


def to_side(value):
    return to_island(value, lambda y, side: (y, 1 - side))


def to_core(value):
    return lax.ppermute(value, "fsdp", fsdp_perm(lambda h, x, c: (h, x, 1 - c)))


def after(value, earlier):
    return lax.optimization_barrier((value, earlier))[0]


def phase(*values):
    return lax.optimization_barrier(values)


def cost(flops, size):
    return pl.CostEstimate(
        flops=int(flops * COST), bytes_accessed=int(size * COST), transcendentals=0
    )


def params(mib):
    return pltpu.CompilerParams(vmem_limit_bytes=mib * MIB)


def term(tok, kc):
    return lax.dot_general(tok, kc, (((0,), (0,)), ((), ())), preferred_element_type=jnp.float32)


def chip_terms(order, side, tokens, kc, their_tokens, their_kc):
    rows, width = kc.shape
    pieces = [(0, 0, BLK), (1, 0, BLK), (2, 0, HALF), (2, HALF, HALF), (3, 0, BLK)]
    count = len(pieces)

    def body(order_ref, tok_ref, kc_ref, their_tok_ref, their_kc_ref, *rest):
        outs, held, sems = rest[:count], rest[count], rest[count + 1]

        def copies(block):
            return [
                pltpu.make_async_copy(held.at[k, pl.ds(start, size)], outs[n], sems.at[n])
                for n, (k, start, size) in enumerate(pieces)
                if block is None or k == block
            ]

        j = pl.program_id(0)
        total = term(tok_ref[...], kc_ref[...])
        total += term(their_tok_ref[...], their_kc_ref[...])
        total = total.astype(jnp.bfloat16)
        for k in range(4):

            @pl.when(j == k)
            def _():
                held[k] = total
                for copy in copies(k):
                    copy.start()

        @pl.when(j == 3)
        def _():
            for copy in copies(None):
                copy.wait()

    whole = pl.BlockSpec((rows, width), lambda j, order: (0, 0))
    columns = pl.BlockSpec((rows, BLK), lambda j, order: (0, block_at(order[0], side, j)))
    return pl.pallas_call(
        body,
        grid_spec=pltpu.PrefetchScalarGridSpec(
            num_scalar_prefetch=1,
            grid=(4,),
            in_specs=[columns, whole, columns, whole],
            out_specs=[pl.BlockSpec(memory_space=pl.ANY)] * count,
            scratch_shapes=[
                pltpu.VMEM((4, BLK, width), jnp.bfloat16),
                pltpu.SemaphoreType.DMA((count,)),
            ],
        ),
        out_shape=[jax.ShapeDtypeStruct((size, width), jnp.bfloat16) for _, _, size in pieces],
        compiler_params=params(TERM_MIB),
        cost_estimate=cost(2 * 8 * rows * BLK * width, 12 * MIB),
        name="chip_terms",
    )(order, tokens, kc, their_tokens, their_kc)


def walk(j):
    return j ^ (j >> 1)


def side_products(order, side, first, kc, their_kc, blocks, grads):
    rows, width = kc.shape
    count = len(blocks)

    def body(order_ref, kc_ref, their_kc_ref, *rest):
        out_ref, theirs_ref = rest[-2:]
        j = pl.program_id(0)
        for k in range(count):

            @pl.when(j == k)
            def _():
                block = rest[k][...]
                for kc_rows, ref in ((kc_ref, out_ref), (their_kc_ref, theirs_ref.at[0])):
                    ref[...] = lax.dot_general(
                        kc_rows[...],
                        block,
                        (((1,), (1,)), ((), ())),
                        preferred_element_type=jnp.float32,
                    ).astype(jnp.bfloat16)

    def whole(shape):
        return pl.BlockSpec(shape, lambda j, order: (0,) * len(shape))

    operands = [order, kc, their_kc, *blocks]
    in_specs = [whole((rows, width))] * 2 + [whole((BLK, width))] * count
    aliases = {}
    if grads is not None:
        aliases = {len(operands): 0}
        operands.append(grads)
        in_specs.append(pl.BlockSpec(memory_space=pl.ANY))
    return pl.pallas_call(
        body,
        grid_spec=pltpu.PrefetchScalarGridSpec(
            num_scalar_prefetch=1,
            grid=(count,),
            in_specs=in_specs,
            out_specs=[
                pl.BlockSpec(
                    (rows, BLK), lambda j, order: (0, block_at(order[0], side, walk(first + j)))
                ),
                pl.BlockSpec((1, rows, BLK), lambda j, order: (j, 0, 0)),
            ],
        ),
        out_shape=[
            jax.ShapeDtypeStruct((rows, 16 * BLK), jnp.bfloat16),
            jax.ShapeDtypeStruct((count, rows, BLK), jnp.bfloat16),
        ],
        input_output_aliases=aliases,
        compiler_params=params(INPUT_MIB),
        cost_estimate=cost(4 * count * rows * BLK * width, 2 * count * MIB),
        name="side_products",
    )(*operands)


def put_blocks(order, grads, *arrived):
    counts = [part.shape[0] for part in arrived]
    pieces = [(group, k) for group, count in enumerate(counts) for k in range(count)]

    def body(order_ref, *rest):
        out_ref, sems = rest[-2:]
        copies = []
        for n, (group, k) in enumerate(pieces):
            place = block_at(order_ref[0] ^ 1, n // 4, walk(n % 4))
            copies.append(
                pltpu.make_async_copy(
                    rest[group].at[k],
                    out_ref.at[:, pl.ds(pl.multiple_of(place * BLK, BLK), BLK)],
                    sems.at[n],
                )
            )
        for copy in copies:
            copy.start()
        for copy in copies:
            copy.wait()

    return pl.pallas_call(
        body,
        grid_spec=pltpu.PrefetchScalarGridSpec(
            num_scalar_prefetch=1,
            grid=(1,),
            in_specs=[
                *[pl.BlockSpec(part.shape, lambda j, order: (0, 0, 0)) for part in arrived],
                pl.BlockSpec(memory_space=pl.ANY),
            ],
            out_specs=pl.BlockSpec(memory_space=pl.ANY),
            scratch_shapes=[pltpu.SemaphoreType.DMA((len(pieces),))],
        ),
        out_shape=jax.ShapeDtypeStruct(grads.shape, jnp.bfloat16),
        input_output_aliases={1 + len(arrived): 0},
        compiler_params=params(INPUT_MIB),
        cost_estimate=cost(0, 6 * MIB),
        name="put_blocks",
    )(order, *arrived, grads)


def dequantize(codes, exponents):
    rows, blocks = exponents.shape
    size = codes.shape[1] // blocks

    def body(codes_ref, exponents_ref, out_ref):
        scales = jnp.exp2(exponents_ref[...].astype(jnp.float32))
        for k in range(blocks):
            part = codes_ref[:, k * size : (k + 1) * size].astype(jnp.float32)
            out_ref[:, k * size : (k + 1) * size] = (part * scales[:, k : k + 1]).astype(
                jnp.bfloat16
            )

    return pl.pallas_call(
        body,
        out_shape=jax.ShapeDtypeStruct(codes.shape, jnp.bfloat16),
        compiler_params=params(INPUT_MIB),
        cost_estimate=cost(2 * rows * codes.shape[1], 2 * MIB),
        name="dequantize",
    )(codes, exponents)


def add_blocks(*blocks):
    rows, width = blocks[0].shape
    step = rows // 2

    def body(*refs):
        total = refs[0][...].astype(jnp.float32)
        for ref in refs[1:-1]:
            total = total + ref[...].astype(jnp.float32)
        refs[-1][...] = total.astype(jnp.bfloat16)

    spec = pl.BlockSpec((step, width), lambda j: (j, 0))
    return pl.pallas_call(
        body,
        grid=(2,),
        in_specs=[spec] * len(blocks),
        out_specs=spec,
        out_shape=jax.ShapeDtypeStruct((rows, width), jnp.bfloat16),
        compiler_params=params(INPUT_MIB),
        cost_estimate=cost(len(blocks) * rows * width, 2 * (len(blocks) + 1) * rows * width),
        name="add_blocks",
    )(*blocks)


def plain_kernel(body, shapes, name, *operands):
    return pl.pallas_call(
        body,
        out_shape=[jax.ShapeDtypeStruct(shape, jnp.bfloat16) for shape in shapes],
        compiler_params=params(INPUT_MIB),
        cost_estimate=cost(0, 6 * MIB),
        name=name,
    )(*operands)


def rounded_sum(*parts):
    total = parts[0].astype(jnp.float32)
    for part in parts[1:]:
        total = total + part.astype(jnp.float32)
    return total.astype(jnp.bfloat16)


def pair_copies(own, other):
    rows, width = own.shape

    def body(own_ref, other_ref, out_ref):
        total = rounded_sum(own_ref[...], other_ref[...])
        for k in range(4):
            out_ref[k] = total

    return plain_kernel(body, [(4, rows, width)], "pair_copies", own, other)[0]


def relay_away(one, three, from_left, from_right, low, high):
    width = one.shape[1]

    def body(one_ref, three_ref, left_ref, right_ref, low_ref, high_ref, plus_ref, minus_ref):
        plus_ref[:HALF] = rounded_sum(one_ref[:HALF], left_ref[...])
        plus_ref[HALF:BLK] = one_ref[HALF:]
        plus_ref[BLK:] = low_ref[...]
        minus_ref[:HALF] = three_ref[:HALF]
        minus_ref[HALF:BLK] = rounded_sum(three_ref[HALF:], right_ref[...])
        minus_ref[BLK:] = high_ref[...]

    shapes = [(BLK + HALF, width)] * 2
    return plain_kernel(
        body, shapes, "relay_away", one, three, from_left, from_right, low, high
    )


def relay_home(kept, from_left, from_right, one, three):
    width = kept.shape[1]

    def body(kept_ref, left_ref, right_ref, one_ref, three_ref, sum_ref, plus_ref, minus_ref):
        sum_ref[...] = rounded_sum(kept_ref[...], left_ref[:BLK], right_ref[:BLK])
        plus_ref[:HALF] = rounded_sum(one_ref[:HALF], left_ref[BLK:])
        plus_ref[HALF:] = one_ref[HALF:]
        minus_ref[:HALF] = three_ref[:HALF]
        minus_ref[HALF:] = rounded_sum(three_ref[HALF:], right_ref[BLK:])

    return plain_kernel(
        body, [(BLK, width)] * 3, "relay_home", kept, from_left, from_right, one, three
    )


def local(
    tokens,
    key_cotangent,
    local_keys,
    pseudo_codes,
    code_exponents,
    outer_weights,
    outer_momentum,
    fragment,
):
    place = lax.axis_index("fsdp")
    here = place.astype(jnp.int32).reshape(1)

    own = local_keys[0, local_keys.shape[1] - 1]
    their_kc = to_core(key_cotangent)
    their_tokens = to_core(tokens)
    left = to_x(own, 1)
    right = to_x(own, -1)
    peer = to_z(own)
    delta = dequantize(pseudo_codes[0], after(code_exponents[0], own))
    far = to_x(after(own, (delta, their_kc)), 2)
    other_delta = to_side(delta)

    away = chip_terms(here, 1, tokens, key_cotangent, their_tokens, after(their_kc, delta))
    left, right, peer, delta = after((left, right, peer, delta), away[0])

    low, high = after((away[2], away[3]), (left, right, peer))
    from_left = to_x(low, 1)
    from_right = to_x(high, -1)
    peer_left = to_z(left)
    home = chip_terms(here, 0, tokens, key_cotangent, their_tokens, after(their_kc, (peer, right)))
    peer_right = to_z(after(right, (home[0], peer_left)))
    from_left, from_right, away, home, far, own, other_delta = phase(
        from_left, from_right, away, home, far, own, other_delta
    )
    plus, minus = relay_away(away[1], away[4], from_left, from_right, home[2], home[3])

    away_left = to_x(plus, 1)
    away_right = to_x(minus, -1)
    peer_far = to_z(after(far, peer_left))
    pairs = over_y(pair_copies(after(delta, plus), other_delta))
    near = [own, right, left, far]
    grads, near_theirs = side_products(
        here, 0, 0, key_cotangent, after(their_kc, plus), near, None
    )
    away_left, away_right, peer_right, grads, near_theirs = phase(
        away_left, away_right, peer_right, grads, near_theirs
    )

    away_sum, plus, minus = relay_home(away[0], away_left, away_right, home[1], home[4])
    home_left = to_x(plus, 1)
    home_right = to_x(minus, -1)
    crossed = to_z(away_sum)
    near_there = to_core(after(near_theirs, peer_far))
    across = after([peer, peer_right, peer_left, peer_far], away_sum)
    grads, across_theirs = side_products(here, 1, 0, key_cotangent, their_kc, across, grads)
    across_there = to_core(after(across_theirs, (home_left, home_right, crossed)))
    pairs = after(pairs, grads)
    mean_delta = jnp.sum(pairs.astype(jnp.float32), axis=0) / ISLANDS
    new_momentum = momentum_rate * outer_momentum + mean_delta
    new_weights = outer_weights - outer_rate * (mean_delta + momentum_rate * new_momentum)
    chosen = lax.dynamic_index_in_dim(local_keys[0], fragment[0], 0, keepdims=False)
    synced_keys = (
        keep_share * chosen.astype(jnp.float32) + (1.0 - keep_share) * new_weights
    ).astype(jnp.bfloat16)[None]
    input_grads = put_blocks(here, after(grads, synced_keys), near_there, across_there)
    home_kept = after(home[0], input_grads)
    weight_grads = add_blocks(home_kept, home_left, home_right, crossed)[None]
    return (input_grads, weight_grads, new_weights, new_momentum, synced_keys)


def solution(mesh):
    placed = (
        P(("island", "fsdp"), None),
        P(("island", "fsdp"), None),
        P("island", None, "fsdp", None),
        P("island", "fsdp", None),
        P("island", "fsdp", None),
        P("fsdp", None),
        P("fsdp", None),
        P("island"),
    )
    return jax.shard_map(
        local,
        mesh=mesh,
        in_specs=placed,
        out_specs=(
            P(("island", "fsdp"), None),
            P("island", "fsdp", None),
            P("fsdp", None),
            P("fsdp", None),
            P("island", "fsdp", None),
        ),
        check_vma=False,
    )
```
